256 devices in a mesh: tm: 64 (over z, x, core), space: 4 (over y).
Axes of the slice: x: 4, y: 4, z: 8, core: 2. Of those that a mesh axis runs over, the one named last changes fastest.
Arguments:
- initial: float32 [256, 512], P('space'), may hold values from -6 to 6
- diffusivity: float32 [256, 512], P('space'), may hold values from 0.0008 to 0.0035
- forcing: float32 [1024, 256, 512], P('tm', 'space'), may hold values from -3 to 3
- guessed: float32 [256, 256, 512], P('tm', 'space'), may hold values from -6 to 6
Outputs:
- c_states: float32 [256, 256, 512], P('tm', 'space')
The draws below stay inside these ranges and needn't reach their ends.
All inputs are finite; a program needn't handle non-finite values.
Results may differ from the reference program's by a relative error of at most 0.00002.
Values sent between devices are 32-bit elements; how exact they have to be, the bound alone decides.
No kernel may reach another device: no remote copies, remote signals or barrier semaphores. Data moves between devices by JAX's collectives and lax.ppermute only.
A program may use at most 64 MiB of HBM per device.

```python
import math
import jax
import jax.numpy as jnp
from jax import lax

NY = 512
FACTOR = 4
NX = 256
TSTEPS = 1024
CPOINTS = 256


def draw_forcing(key, part):
    key = jax.random.fold_in(key, 17)
    extent = (TSTEPS, NX, NY)
    values = 0.3 * jax.random.normal(key, extent, jnp.float32)
    return jnp.clip(values, -3.0, 3.0)


def block_scale(key, shape, pieces, least, top_value):
    def one(dim, parts):
        steps = jax.random.uniform(jax.random.fold_in(jax.random.fold_in(key, 6), dim), (parts,), jnp.float32, least / len(pieces), top_value / len(pieces))
        return jnp.repeat(jnp.exp(steps), shape[dim] // parts).reshape((-1,) + (1,) * (len(shape) - dim - 1))

    level = one(*pieces[0])
    for cut in pieces[1:]:
        level = level * one(*cut)
    return level


def normal_values(own_key, dims, spread, limit, shards=(), held_as=jnp.bfloat16):
    entries = spread * jax.random.normal(own_key, dims, jnp.float32)
    if shards:
        entries = entries * block_scale(own_key, dims, shards, -0.22, 0.18)
    return jnp.clip(entries, -limit, limit).astype(held_as)


def setup_inputs(seed: int = 0) -> dict:
    streams_of = jax.random.split(jax.random.key(seed), 5)
    return {
        "initial": normal_values(streams_of[0], (NX, NY), 1.0, 6.0, ((0, 4),), jnp.float32),
        "diffusivity": jnp.clip(jnp.exp(math.log(0.0035) - 1.4759066 * jax.random.uniform(streams_of[1], (NX, NY), jnp.float32) ** block_scale(streams_of[1], (NX, NY), ((0, 4),), -0.2, 0.2)), 0.0008, 0.0035),
        "forcing": draw_forcing(jax.random.fold_in(streams_of[4], 71), 0),
        "guessed": normal_values(streams_of[3], (CPOINTS, NX, NY), 1.0, 6.0, ((0, 64), (1, 4)), jnp.float32),
    }


def laplace(fields):
    padding = [(0, 0)] * (fields.ndim - 2) + [(1, 1), (1, 1)]
    padded = jnp.pad(fields, padding)
    return padded[..., 2:, 1:-1] + padded[..., :-2, 1:-1] + padded[..., 1:-1, 2:] + padded[..., 1:-1, :-2] - 4.0 * fields


def advance(fields, diffusivity, stride):
    return fields + (stride * diffusivity) * laplace(fields)


def march_on(starts, sources, number, diffusivity, stride):
    values = []
    current = starts
    for i in range(number):
        current = advance(current, diffusivity, stride) + sources[:, i]
        values.append(current)
    return values


def relax_level(sources, guesses, leading, diffusivity, stride):
    starts = jnp.concatenate([leading[None], guesses[:-1]], 0)
    relaxed = march_on(starts, sources, FACTOR, diffusivity, stride)[-1]
    starts = jnp.concatenate([leading[None], relaxed[:-1]], 0)
    before = march_on(starts, sources, FACTOR - 1, diffusivity, stride)[-1]
    residual = sources[:, -1] + advance(before, diffusivity, stride) - relaxed
    return relaxed, residual


def interpolate(sources, corrected, diffusivity, stride):
    starts = jnp.concatenate([jnp.zeros_like(corrected[:1]), corrected[:-1]], 0)
    values = march_on(starts, sources, FACTOR - 1, diffusivity, stride)
    stacked = jnp.stack(values + [corrected], 1)
    return stacked.reshape((-1,) + corrected.shape[1:])


def reference(initial, diffusivity, forcing, guessed):
    empty_state = jnp.zeros_like(initial)
    source_zero = forcing.reshape((-1, FACTOR) + initial.shape)
    relaxed_zero, residual_zero = relax_level(source_zero, guessed, initial, diffusivity, 1.0)
    source_one = residual_zero.reshape((-1, FACTOR) + initial.shape)
    relaxed_one, residual_one = relax_level(source_one, jnp.zeros_like(source_one[:, 0]), empty_state, diffusivity, float(FACTOR))
    source_two = residual_one.reshape((-1, FACTOR) + initial.shape)
    relaxed_two, residual_two = relax_level(source_two, jnp.zeros_like(source_two[:, 0]), empty_state, diffusivity, float(FACTOR ** 2))

    def coarse_step(current, source):
        current = advance(current, diffusivity, float(FACTOR ** 3)) + source
        return current, current

    final_state, coarsest = lax.scan(coarse_step, empty_state, residual_two)
    errors_two = interpolate(source_two, relaxed_two + coarsest, diffusivity, float(FACTOR ** 2))
    errors_one = interpolate(source_one, relaxed_one + errors_two, diffusivity, float(FACTOR))
    return relaxed_zero + errors_one
```

```python
import jax
import jax.numpy as jnp
from jax import lax
from jax.sharding import PartitionSpec as P

FACTOR = 4
E = 32
S0, S1, S2, S3 = 1.0, 4.0, 16.0, 64.0


def wide(v, e):
    pads = [(0, 0)] * (v.ndim - 2) + [(e, e), (0, 0)]
    return jnp.pad(v, pads)


def regrow(v, before, after):
    return wide(v, after - before)


def ring(axis, by):
    n = lax.axis_size(axis)
    return [(i, (i + by) % n) for i in range(n)]


def shift(v, axis, by):
    return lax.ppermute(v, axis, ring(axis, by))


def swap(v, bit):
    n = lax.axis_size("tm")
    return lax.ppermute(v, "tm", [(i, i ^ bit) for i in range(n)])


def per_device(initial, diffusivity, forcing, guessed):
    p = lax.axis_index("tm")
    y = lax.axis_index("space")
    ny = lax.axis_size("space")
    rows = diffusivity.shape[0]
    z, x, c = p // 8, (p // 2) % 4, p % 2
    h = x // 2
    odd = x % 2 == 1
    zero = jnp.float32(0)

    above = shift(diffusivity[rows - E :], "space", 1)
    below = shift(diffusivity[:E], "space", -1)
    above = jnp.where(y == 0, zero, above)
    below = jnp.where(y == ny - 1, zero, below)
    dwide = jnp.concatenate([above, diffusivity, below], 0)

    def step(v, s):
        e = (v.shape[-2] - rows) // 2
        d = dwide[E - e : E + rows + e]
        q = jnp.pad(v, [(0, 0)] * (v.ndim - 2) + [(1, 1), (1, 1)])
        lap = q[..., 2:, 1:-1] + q[..., :-2, 1:-1] + q[..., 1:-1, 2:] + q[..., 1:-1, :-2] - 4.0 * v
        return v + (s * d) * lap

    def steps(v, s, k):
        for _ in range(k):
            v = step(v, s)
        return v

    sources = forcing.reshape((FACTOR, FACTOR) + forcing.shape[1:])
    first = jnp.where(p == 0, initial, zero)[None]
    cur = wide(jnp.concatenate([first, guessed], 0), 8)
    src = wide(jnp.concatenate([sources, jnp.zeros_like(sources[:1])], 0), 8)
    for i in range(FACTOR):
        cur = step(cur, S0) + src[:, i]
    relaxed, gw = cur[:4], cur[4]
    d = relaxed - wide(guessed, 8)
    dw = regrow(d, 8, 16)
    gw16 = regrow(gw, 8, 16)
    xf = step(dw[0], S1) + dw[1]
    xf = step(xf, S1) + dw[2]
    yf = steps(step(dw[3], S1) + gw16, S1, 2)
    xy = steps(jnp.stack([xf, yf]), S0, 4)
    theirs = swap(xy, 1)
    x0 = jnp.where(c == 0, xy[0], theirs[0])
    x1 = jnp.where(c == 0, theirs[0], xy[0])
    y0 = jnp.where(c == 0, xy[1], theirs[1])
    y1 = jnp.where(c == 0, theirs[1], xy[1])
    r = x1 + y0

    even_field = step(step(x0, S2) + r, S2) + y1
    odd_field = steps(step(r, S2) + y1, S2, 2)
    f = jnp.where(odd, jnp.where(c == 0, x0, odd_field), jnp.where(c == 0, even_field, zero))
    role_b = (h == 0) & (c == 0)
    role_t = ((h == 1) & (c == 0)) | ((x == 1) & (c == 1))
    role_a = (x == 3) & (c == 1)

    def to_psi(v):
        g1 = step(v, S3)
        g2 = step(g1, S3)
        return jnp.where(role_b, g2, jnp.where(role_t, g1, v))

    psi = to_psi(f)
    f1 = jnp.where(z >= 1, shift(f, "tm", 8), zero)
    psi2 = jnp.where(z >= 2, shift(psi, "tm", 16), zero)
    q0 = (z == 0) & (x == 0)
    d3gw = shift(jnp.stack([dw[3], gw16])[:, 8:-8], "tm", 1)
    d3gw = jnp.where(p == 0, zero, d3gw)
    ry = shift(jnp.stack([r, y1]), "tm", 2)
    ry = jnp.where(q0, zero, ry)
    rp, yp = ry[0], ry[1]

    psi1 = to_psi(f1)
    u = regrow(psi2, 16, 24)
    u = steps(u, S3, 2) + regrow(psi1, 16, 24)
    u = steps(u, S3, 2) + regrow(psi, 16, 24)
    u2 = jnp.where(z >= 2, shift(u, "tm", 16), zero)
    u5 = jnp.where(z >= 5, shift(u, "tm", 40), zero)
    eps = regrow(u2, 24, 32) + steps(regrow(u5, 24, 32), S3, 6)
    f1w, fw = regrow(f1, 16, 32), regrow(f, 16, 32)
    eps = eps + jnp.where(role_b, f1w, zero)
    tau = jnp.where(role_t, f1w, zero)
    alpha = jnp.where(role_a, f1w, zero)
    b0 = jnp.where(role_b, fw, zero)
    b1 = jnp.where(role_t, fw, zero)
    eps1 = step(eps, S3) + tau
    tau1 = b0 + alpha
    eps2 = step(eps1, S3) + tau1
    tau2 = b1
    zs = steps(jnp.stack([eps, eps1, eps2]), S2, 4) + jnp.stack([tau, tau1, tau2])

    mine = jnp.where(c == 0, zs[:2], zs[1:])
    other = jnp.where(c == 0, zs[1:], zs[:2])
    mine = mine + swap(other, 1)
    keep = jnp.where(h == 0, mine[0], mine[1])
    give = jnp.where(h == 0, mine[1], mine[0])
    keep = keep + swap(give, 4)
    s1 = step(rp, S2) + jnp.where(c == 0, xy[0], x0) + yp
    moved = jnp.where(c == 0, steps(keep, S2, 2), keep)
    give = jnp.where(odd, keep, jnp.where(c == 0, moved + regrow(s1, 16, 32), moved))
    keep = jnp.where(odd, moved, keep) + swap(give, 2)

    n = rows + 2 * E
    from_above = shift(keep[n - 40 :], "space", 1)
    from_below = shift(keep[:40], "space", -1)
    from_above = jnp.where(y == 0, zero, from_above)
    from_below = jnp.where(y == ny - 1, zero, from_below)
    zfull = keep[E - 8 : E + rows + 8] + jnp.concatenate([from_above, from_below], 0)
    zother = swap(zfull, 1)
    qf = jnp.where(c == 0, zfull, zother)
    both = steps(jnp.stack([qf, zfull]), S1, 4)
    q, zn = both[0], both[1]
    qa = step(q, S2)
    e2a = jnp.where(c == 0, q, qa)
    e2b = jnp.where(c == 0, qa, jnp.where(odd, zn, step(qa, S2)))
    t1 = step(e2a, S1)
    t2 = step(t1, S1)
    t3 = step(t2, S1)
    correction = jnp.stack([t1, t2, t3, e2b])[:, 8:-8]

    r24, x024, yp24, rp24 = (regrow(v, 16, 24) for v in (r, x0, yp, rp))
    d3p, gwp = regrow(d3gw[0], 8, 24), regrow(d3gw[1], 8, 24)
    d0 = regrow(d[0], 8, 24) + gwp
    quad = steps(jnp.stack([d3p, d0, regrow(d[1], 8, 24)]), S0, 4)
    a3p, a0, a1 = quad[0], quad[1], quad[2]
    rprev = jnp.where(c == 0, rp24, x024 + yp24)
    rown = jnp.where(c == 0, x024 + yp24, r24)
    pair = steps(jnp.stack([rp24, step(rp24, S2) + x024 + yp24]), S1, 4)
    ea = jnp.where(c == 0, zero, pair[0])
    eb = jnp.where(c == 0, pair[0], jnp.where(odd, zero, pair[1]))
    y_1 = step(rprev + ea, S1) + a3p
    y_2 = step(y_1, S1) + a0
    y_3 = step(y_2, S1) + a1
    rel = regrow(relaxed, 8, 24)
    local = jnp.stack([rel[0] + gwp + y_1, rel[1] + y_2, rel[2] + y_3, rel[3] + rown + eb])
    m = rows + 48
    la = shift(local[:, m - 24 :], "space", 1)
    lb = shift(local[:, :24], "space", -1)
    la = jnp.where(y == 0, zero, la)
    lb = jnp.where(y == ny - 1, zero, lb)
    inner = local[:, 24:-24]
    inner = inner + jnp.pad(la, ((0, 0), (0, rows - 24), (0, 0))) + jnp.pad(lb, ((0, 0), (rows - 24, 0), (0, 0)))
    return inner + correction


def solution(mesh):
    return jax.shard_map(
        per_device,
        mesh=mesh,
        in_specs=(
            P("space", None),
            P("space", None),
            P("tm", "space", None),
            P("tm", "space", None),
        ),
        out_specs=P("tm", "space", None),
        check_vma=False,
    )
```

```python
import jax
import jax.numpy as jnp
from jax import lax
from jax.sharding import PartitionSpec as P

FACTOR = 4
E = 32
EDGE = 64
S0, S1, S2, S3 = 1.0, 4.0, 16.0, 64.0


def wide(v, e):
    return jnp.pad(v, [(0, 0)] * (v.ndim - 2) + [(e, e), (0, 0)])


def regrow(v, before, after):
    return wide(v, after - before)


def edged(v):
    return jnp.pad(v, [(0, 0)] * (v.ndim - 1) + [(EDGE, EDGE)])


def shift(v, axis, by):
    n = lax.axis_size(axis)
    return lax.ppermute(v, axis, [(i, (i + by) % n) for i in range(n)])


def swap(v, bit):
    n = lax.axis_size("tm")
    return lax.ppermute(v, "tm", [(i, i ^ bit) for i in range(n)])


def hold(*values):
    return lax.optimization_barrier(values)


def step(v, d, s):
    q = jnp.pad(v, [(0, 0)] * (v.ndim - 2) + [(1, 1), (1, 1)])
    lap = q[..., 2:, 1:-1] + q[..., :-2, 1:-1] + q[..., 1:-1, 2:] + q[..., 1:-1, :-2] - 4.0 * v
    return v + (s * d) * lap


def steps(v, d, s, k):
    for _ in range(k):
        v = step(v, d, s)
    return v


def per_device(initial, diffusivity, forcing, guessed):
    p = lax.axis_index("tm")
    y = lax.axis_index("space")
    ny = lax.axis_size("space")
    rows, columns = diffusivity.shape
    z, x, c = p // 8, (p // 2) % 4, p % 2
    h = x // 2
    odd = x % 2 == 1
    core0 = c == 0
    zero = jnp.float32(0)

    sources = forcing.reshape((FACTOR, FACTOR) + forcing.shape[1:])
    first = jnp.where(p == 0, initial, zero)[None]
    cur = wide(jnp.concatenate([first, guessed], 0), 8)
    src = wide(jnp.concatenate([sources, jnp.zeros_like(sources[:1])], 0), 8)
    above = shift(diffusivity[rows - E :], "space", 1)
    below = shift(diffusivity[:E], "space", -1)
    above, below, cur, src = hold(above, below, cur, src)
    above = jnp.where(y == 0, zero, above)
    below = jnp.where(y == ny - 1, zero, below)
    dwide = jnp.concatenate([above, diffusivity, below], 0)

    def dext(e):
        return dwide[E - e : E + rows + e]

    for i in range(FACTOR):
        cur = step(cur, dext(8), S0) + src[:, i]
    relaxed, gw = cur[:4], cur[4]
    d = relaxed - wide(guessed, 8)
    dw = regrow(d, 8, 16)
    gw16 = regrow(gw, 8, 16)
    d16 = dext(16)
    xf = step(dw[0], d16, S1) + dw[1]
    xf = step(xf, d16, S1) + dw[2]
    yf = steps(step(dw[3], d16, S1) + gw16, d16, S1, 2)
    xy = steps(jnp.stack([xf, yf]), d16, S0, 4)
    theirs = swap(xy, 1)

    dpad = edged(dwide)
    dhalf = jnp.where(core0, dpad[:, :384], dpad[:, 256:])
    dquarter = jnp.where(odd, dhalf[:, 128:], dhalf[:, :256])

    def half(v):
        w = edged(v)
        return jnp.where(core0, w[..., :384], w[..., 256:])

    mine_h, theirs_h = half(xy), half(theirs)
    x0 = jnp.where(core0, mine_h[0], theirs_h[0])
    x1 = jnp.where(core0, theirs_h[0], mine_h[0])
    y0 = jnp.where(core0, mine_h[1], theirs_h[1])
    y1 = jnp.where(core0, theirs_h[1], mine_h[1])
    r = x1 + y0
    dh = dhalf[E - 16 : E + rows + 16]
    t = step(jnp.where(odd, r, x0), dh, S2) + jnp.where(odd, y1, r)
    t = step(t, dh, S2)
    f1 = jnp.where(odd, x0, t + y1)
    f2 = jnp.where(odd, step(t, dh, S2), zero)
    ff = jnp.stack([f1, f2])
    keep = jnp.where(odd, ff[..., 128:], ff[..., :256])
    give = jnp.where(odd, ff[..., :256], ff[..., 128:])
    keep = keep + swap(give, 2)

    def dq(e):
        return dquarter[E - e : E + rows + e]

    def to_psi(v):
        g = step(v[0], dq(16), S3) + v[1]
        return jnp.where(h == 0, step(g, dq(16), S3), g)

    psi = to_psi(keep)
    xy0 = jnp.where(core0, xy, theirs)
    xy1 = jnp.where(core0, theirs, xy)
    rfull = xy1[0] + xy0[1]
    ry = jnp.where(core0, rfull, xy[1])
    before, psi2, ry = hold(shift(keep, "tm", 8), shift(psi, "tm", 16), shift(ry, "tm", 2))
    before = jnp.where(z >= 1, before, zero)
    psi2 = jnp.where(z >= 2, psi2, zero)
    psi1 = to_psi(before)
    u = steps(regrow(psi2, 16, 24), dq(24), S3, 2) + regrow(psi1, 16, 24)
    u = steps(u, dq(24), S3, 2) + regrow(psi, 16, 24)
    u2, u5, d3gw, ry2 = hold(
        shift(u, "tm", 16),
        shift(u, "tm", 40),
        shift(jnp.stack([dw[3], gw16])[:, 8:-8], "tm", 1),
        swap(ry, 1),
    )
    u2 = jnp.where(z >= 2, u2, zero)
    u5 = jnp.where(z >= 5, u5, zero)
    q0 = (z == 0) & (x == 0)
    d3gw = jnp.where(p == 0, zero, d3gw)
    rp = jnp.where(q0, zero, jnp.where(core0, ry, ry2))
    yp = jnp.where(q0, zero, jnp.where(core0, ry2, ry))
    s1 = step(rp, d16, S2) + xy0[0] + yp

    dz = dq(32)
    eps = regrow(u2, 24, 32) + steps(regrow(u5, 24, 32), dz, S3, 6)
    bw, kw = regrow(before, 16, 32), regrow(keep, 16, 32)
    low = h == 0
    eps = eps + jnp.where(low, bw[0], zero)
    tau = jnp.where(low, bw[1], bw[0])
    alpha = jnp.where(low, zero, bw[1])
    b0 = jnp.where(low, kw[0], zero)
    tau2 = jnp.where(low, kw[1], kw[0])
    eps1 = step(eps, dz, S3) + tau
    tau1 = b0 + alpha
    eps2 = step(eps1, dz, S3) + tau1
    zs = steps(jnp.stack([eps, eps1, eps2]), dz, S2, 4) + jnp.stack([tau, tau1, tau2])
    zs = zs[..., EDGE:-EDGE]
    keep = jnp.where(low, zs[:2], zs[1:])
    give = jnp.where(low, zs[1:], zs[:2])
    other, s1x = hold(swap(give, 4), swap(s1, 2))
    keep = keep + other

    def r24(v):
        return regrow(v, 16, 24)

    d24 = dext(24)
    s1q = jnp.where(odd, r24(s1x), zero)
    d3p, gwp = regrow(d3gw[0], 8, 24), regrow(d3gw[1], 8, 24)
    d0 = regrow(d[0], 8, 24) + gwp
    quad = steps(jnp.stack([d3p, d0, regrow(d[1], 8, 24)]), d24, S0, 4)
    a3p, a0, a1 = quad[0], quad[1], quad[2]
    rprev = jnp.where(core0, r24(rp), r24(xy0[0] + yp))
    rown = jnp.where(core0, r24(xy0[0] + yp), r24(rfull))
    ea = jnp.where(core0, s1q, step(s1q, d24, S2) + r24(rp))
    eb = step(ea, d24, S2) + rprev
    eb = jnp.where(odd & (c == 1), zero, eb)
    pair = steps(jnp.stack([ea, eb]), d24, S1, 4)
    y_1 = step(rprev + pair[0], d24, S1) + a3p
    y_2 = step(y_1, d24, S1) + a0
    y_3 = step(y_2, d24, S1) + a1
    rel = regrow(relaxed, 8, 24)
    local = jnp.stack([rel[0] + gwp + y_1, rel[1] + y_2, rel[2] + y_3, rel[3] + rown + pair[1]])

    n = rows + 2 * E
    from_above, from_below = hold(
        shift(keep[:, n - 48 :], "space", 1), shift(keep[:, :48], "space", -1)
    )
    from_above = jnp.where(y == 0, zero, from_above)
    from_below = jnp.where(y == ny - 1, zero, from_below)
    keep = keep[:, 16:-16] + jnp.concatenate([from_above, from_below], 1)
    m = rows + 48
    other, la, lb = hold(
        swap(keep, 2), shift(local[:, m - 24 :], "space", 1), shift(local[:, :24], "space", -1)
    )
    keep = jnp.where(odd, jnp.concatenate([other, keep], 2), jnp.concatenate([keep, other], 2))
    other = swap(keep, 1)
    both = jnp.where(
        core0, jnp.concatenate([keep, other], 2), jnp.concatenate([other, keep], 2)
    )
    both = steps(both, d16, S1, 4)
    q, zn = both[0], both[1]
    q = jnp.where(odd, steps(q, d16, S2, 2), q)
    q = jnp.where(core0, q, step(q, d16, S2))
    e2b = jnp.where(odd & (c == 1), zn, step(q, d16, S2))
    t1 = step(q, d16, S1)
    t2 = step(t1, d16, S1)
    t3 = step(t2, d16, S1)
    correction = jnp.stack([t1, t2, t3, e2b])[:, 16:-16]

    la = jnp.where(y == 0, zero, la)
    lb = jnp.where(y == ny - 1, zero, lb)
    inner = local[:, 24:-24]
    inner = (
        inner
        + jnp.pad(la, ((0, 0), (0, rows - 24), (0, 0)))
        + jnp.pad(lb, ((0, 0), (rows - 24, 0), (0, 0)))
    )
    return inner + correction


def solution(mesh):
    return jax.shard_map(
        per_device,
        mesh=mesh,
        in_specs=(
            P("space", None),
            P("space", None),
            P("tm", "space", None),
            P("tm", "space", None),
        ),
        out_specs=P("tm", "space", None),
        check_vma=False,
    )
```

```python
import jax
import jax.numpy as jnp
from jax import lax
from jax.sharding import PartitionSpec as P

FACTOR = 4
E = 32
EDGE = 64
S0, S1, S2, S3 = 1.0, 4.0, 16.0, 64.0


def wide(v, e):
    return jnp.pad(v, [(0, 0)] * (v.ndim - 2) + [(e, e), (0, 0)])


def regrow(v, before, after):
    return wide(v, after - before)


def edged(v):
    return jnp.pad(v, [(0, 0)] * (v.ndim - 1) + [(EDGE, EDGE)])


def shift(v, axis, by):
    n = lax.axis_size(axis)
    return lax.ppermute(v, axis, [(i, (i + by) % n) for i in range(n)])


def swap(v, bit):
    n = lax.axis_size("tm")
    return lax.ppermute(v, "tm", [(i, i ^ bit) for i in range(n)])


def hold(*values):
    return lax.optimization_barrier(values)


def step(v, d, s):
    q = jnp.pad(v, [(0, 0)] * (v.ndim - 2) + [(1, 1), (1, 1)])
    lap = q[..., 2:, 1:-1] + q[..., :-2, 1:-1] + q[..., 1:-1, 2:] + q[..., 1:-1, :-2] - 4.0 * v
    return v + (s * d) * lap


def steps(v, d, s, k):
    for _ in range(k):
        v = step(v, d, s)
    return v


def per_device(initial, diffusivity, forcing, guessed):
    p = lax.axis_index("tm")
    y = lax.axis_index("space")
    ny = lax.axis_size("space")
    rows, columns = diffusivity.shape
    z, x, c = p // 8, (p // 2) % 4, p % 2
    h = x // 2
    odd = x % 2 == 1
    core0 = c == 0
    zero = jnp.float32(0)

    sources = forcing.reshape((FACTOR, FACTOR) + forcing.shape[1:])
    first = jnp.where(p == 0, initial, zero)[None]
    above = shift(diffusivity[rows - E :], "space", 1)
    below = shift(diffusivity[:E], "space", -1)

    start = jnp.concatenate([first, guessed], 0)

    def march(cur, d, src):
        for i in range(FACTOR):
            nxt = step(cur, d, S0)
            cur = jnp.concatenate([nxt[..., :4, :, :] + src(i), nxt[..., 4:, :, :]], -3)
        return cur

    middle = march(start, diffusivity, lambda i: sources[:, i])
    strips = jnp.stack([wide(start[:, :16], 8)[:, :-8], wide(start[:, 48:], 8)[:, 8:]])
    strip_src = jnp.stack([wide(sources[:, :, :16], 8)[:, :, :-8], wide(sources[:, :, 48:], 8)[:, :, 8:]])
    above, below, middle, strips, strip_src = hold(above, below, middle, strips, strip_src)
    above = jnp.where(y == 0, zero, above)
    below = jnp.where(y == ny - 1, zero, below)
    dwide = jnp.concatenate([above, diffusivity, below], 0)

    def dext(e):
        return dwide[E - e : E + rows + e]

    dstrip = jnp.stack([dwide[E - 8 : E + 16], dwide[E + 48 : E + 72]])[:, None]
    strips = march(strips, dstrip, lambda i: strip_src[:, :, i])
    cur = jnp.concatenate([strips[0, :, :16], middle[:, 8:56], strips[1, :, 8:]], 1)
    relaxed, gw = cur[:4], cur[4]
    d = relaxed - wide(guessed, 8)
    dw = regrow(d, 8, 16)
    gw16 = regrow(gw, 8, 16)
    d16 = dext(16)
    xf = step(dw[0], d16, S1) + dw[1]
    xf = step(xf, d16, S1) + dw[2]
    yf = steps(step(dw[3], d16, S1) + gw16, d16, S1, 2)
    xy = steps(jnp.stack([xf, yf]), d16, S0, 4)
    xy, dheld = hold(xy, dwide)
    theirs = swap(xy, 1)

    dpad = edged(dheld)
    dhalf = jnp.where(core0, dpad[:, :384], dpad[:, 256:])
    dquarter = jnp.where(odd, dhalf[:, 128:], dhalf[:, :256])

    def half(v):
        w = edged(v)
        return jnp.where(core0, w[..., :384], w[..., 256:])

    mine_h, theirs_h = half(xy), half(theirs)
    x0 = jnp.where(core0, mine_h[0], theirs_h[0])
    x1 = jnp.where(core0, theirs_h[0], mine_h[0])
    y0 = jnp.where(core0, mine_h[1], theirs_h[1])
    y1 = jnp.where(core0, theirs_h[1], mine_h[1])
    r = x1 + y0
    dh = dhalf[E - 16 : E + rows + 16]
    t = step(jnp.where(odd, r, x0), dh, S2) + jnp.where(odd, y1, r)
    t = step(t, dh, S2)
    f1 = jnp.where(odd, x0, t + y1)
    f2 = jnp.where(odd, step(t, dh, S2), zero)
    ff = jnp.stack([f1, f2])
    keep = jnp.where(odd, ff[..., 128:], ff[..., :256])
    give = jnp.where(odd, ff[..., :256], ff[..., 128:])
    xy0 = jnp.where(core0, xy, theirs)
    xy1 = jnp.where(core0, theirs, xy)
    rfull = xy1[0] + xy0[1]
    other = swap(give, 2)
    keep = keep + other

    def dq(e):
        return dquarter[E - e : E + rows + e]

    def to_psi(v):
        g = step(v[0], dq(16), S3) + v[1]
        return jnp.where(low, step(g, dq(16), S3), g)

    low = h == 0
    psi = to_psi(keep)
    before, psi2, rpart, d3gw = hold(
        shift(keep, "tm", 8),
        shift(psi, "tm", 16),
        shift(jnp.where(core0, rfull[:48], rfull[48:]), "tm", 2),
        shift(jnp.stack([d[3], gw])[:, 4:-4], "tm", 1),
    )
    before = jnp.where(z >= 1, before, zero)
    psi2 = jnp.where(z >= 2, psi2, zero)
    psi1 = to_psi(before)
    u = steps(regrow(psi2, 16, 20), dq(20), S3, 2) + regrow(psi1, 16, 20)
    u = steps(u, dq(20), S3, 2) + regrow(psi, 16, 20)

    q0 = (z == 0) & (x == 0)
    d3gw = regrow(jnp.where(p == 0, zero, d3gw), 4, 16)
    rpart = jnp.where(q0, zero, rpart)
    yp = step(d3gw[0], d16, S1) + d3gw[1]
    yp = steps(steps(yp, d16, S1, 2), d16, S0, 4)
    ry = jnp.concatenate([yp, rpart], 0)

    dz = dq(32)
    bw, kw = regrow(before, 16, 32), regrow(keep, 16, 32)
    eps = jnp.where(low, bw[0], zero)
    tau = jnp.where(low, bw[1], bw[0])
    tau1 = jnp.where(low, kw[0], bw[1])
    tau2 = jnp.where(low, kw[1], kw[0])
    eps1 = step(eps, dz, S3) + tau
    eps2 = step(eps1, dz, S3) + tau1
    near = steps(jnp.stack([eps, eps1, eps2]), dz, S2, 4) + jnp.stack([tau, tau1, tau2])
    u2, u5, ry2, near = hold(shift(u, "tm", 16), shift(u, "tm", 40), swap(ry, 1), near)
    yp = jnp.where(core0, yp, ry2[:96])
    rother = ry2[96:]
    rp = jnp.where(core0, jnp.concatenate([rpart, rother], 0), jnp.concatenate([rother, rpart], 0))
    s1 = step(rp, d16, S2) + xy0[0] + yp
    u2 = jnp.where(z >= 2, u2, zero)
    u5 = jnp.where(z >= 5, u5, zero)
    far = regrow(u2, 20, 32) + steps(regrow(u5, 20, 32), dz, S3, 6)
    far = steps(far, dz, S2, 4)
    far1 = step(far, dz, S3)
    zs = near + jnp.stack([far, far1, step(far1, dz, S3)])
    zs = zs[..., EDGE:-EDGE]
    keep = jnp.where(low, zs[:2], zs[1:])
    give = jnp.where(low, zs[1:], zs[:2])

    def r24(v):
        return regrow(v, 16, 24)

    d24 = dext(24)
    d3p, gwp = r24(d3gw[0]), r24(d3gw[1])
    d0 = regrow(d[0], 8, 24) + gwp
    quad = steps(jnp.stack([d3p, d0, regrow(d[1], 8, 24)]), d24, S0, 4)
    a3p, a0, a1 = quad[0], quad[1], quad[2]
    rprev = jnp.where(core0, r24(rp), r24(xy0[0] + yp))
    rown = jnp.where(core0, r24(xy0[0] + yp), r24(rfull))
    ea = jnp.where(core0, zero, r24(rp))
    eb = step(ea, d24, S2) + rprev
    eb = jnp.where(odd & (c == 1), zero, eb)
    pair = steps(jnp.stack([ea, eb]), d24, S1, 4)
    y_1 = step(rprev + pair[0], d24, S1) + a3p
    y_2 = step(y_1, d24, S1) + a0
    y_3 = step(y_2, d24, S1) + a1
    rel = regrow(relaxed, 8, 24)
    local = jnp.stack([rel[0] + gwp + y_1, rel[1] + y_2, rel[2] + y_3, rel[3] + rown + pair[1]])

    other, s1x, local = hold(swap(give, 4), swap(s1, 2), local)
    keep = keep + other
    s1x = jnp.where(odd, s1x, zero)

    n = rows + 2 * E

    def packed(v):
        return jnp.concatenate([v[0, :24], v[0, 24:], v[1, :24], v[1, 24:]], 1)

    def unpacked(v):
        return jnp.stack(
            [
                jnp.concatenate([v[:, :128], v[:, 128:256]], 0),
                jnp.concatenate([v[:, 256:384], v[:, 384:]], 0),
            ]
        )

    from_above, from_below = hold(
        shift(jnp.stack([packed(keep[:, n - 48 :]), s1x[-24:]]), "space", 1),
        shift(jnp.stack([packed(keep[:, :48]), s1x[:24]]), "space", -1),
    )
    from_above = jnp.where(y == 0, zero, from_above)
    from_below = jnp.where(y == ny - 1, zero, from_below)
    keep = keep[:, 16:-16] + jnp.concatenate(
        [unpacked(from_above[0]), unpacked(from_below[0])], 1
    )
    s1g = s1x + jnp.pad(from_above[1], ((8, 64), (0, 0))) + jnp.pad(from_below[1], ((64, 8), (0, 0)))
    m = rows + 48
    other, la, lb = hold(
        swap(keep, 2), shift(local[:, m - 24 :], "space", 1), shift(local[:, :24], "space", -1)
    )
    keep = jnp.where(odd, jnp.concatenate([other, keep], 2), jnp.concatenate([keep, other], 2))
    other = swap(keep, 1)
    both = jnp.where(
        core0, jnp.concatenate([keep, other], 2), jnp.concatenate([other, keep], 2)
    )
    q = jnp.where(odd, steps(both[0], d16, S2, 2) + s1g, both[0])
    both = steps(jnp.stack([q, both[1]]), d16, S1, 4)
    q, zn = both[0], both[1]
    q = jnp.where(core0, q, step(q, d16, S2))
    e2b = jnp.where(odd & (c == 1), zn, step(q, d16, S2))
    t1 = step(q, d16, S1)
    t2 = step(t1, d16, S1)
    t3 = step(t2, d16, S1)
    correction = jnp.stack([t1, t2, t3, e2b])[:, 16:-16]

    la = jnp.where(y == 0, zero, la)
    lb = jnp.where(y == ny - 1, zero, lb)
    inner = local[:, 24:-24]
    inner = (
        inner
        + jnp.pad(la, ((0, 0), (0, rows - 24), (0, 0)))
        + jnp.pad(lb, ((0, 0), (rows - 24, 0), (0, 0)))
    )
    return inner + correction


def solution(mesh):
    return jax.shard_map(
        per_device,
        mesh=mesh,
        in_specs=(
            P("space", None),
            P("space", None),
            P("tm", "space", None),
            P("tm", "space", None),
        ),
        out_specs=P("tm", "space", None),
        check_vma=False,
    )
```

```python
import jax
import jax.numpy as jnp
from jax import lax
from jax.sharding import PartitionSpec as P

FACTOR = 4
E = 32
EDGE = 64
S0, S1, S2, S3 = 1.0, 4.0, 16.0, 64.0


def wide(v, e):
    return jnp.pad(v, [(0, 0)] * (v.ndim - 2) + [(e, e), (0, 0)])


def regrow(v, before, after):
    return wide(v, after - before)


def edged(v):
    return jnp.pad(v, [(0, 0)] * (v.ndim - 1) + [(EDGE, EDGE)])


def shift(v, axis, by):
    n = lax.axis_size(axis)
    return lax.ppermute(v, axis, [(i, (i + by) % n) for i in range(n)])


def swap(v, bit):
    n = lax.axis_size("tm")
    return lax.ppermute(v, "tm", [(i, i ^ bit) for i in range(n)])


def hold(*values):
    return lax.optimization_barrier(values)


def step(v, d, s):
    q = jnp.pad(v, [(0, 0)] * (v.ndim - 2) + [(1, 1), (1, 1)])
    lap = q[..., 2:, 1:-1] + q[..., :-2, 1:-1] + q[..., 1:-1, 2:] + q[..., 1:-1, :-2] - 4.0 * v
    return v + (s * d) * lap


def steps(v, d, s, k):
    for _ in range(k):
        v = step(v, d, s)
    return v


def per_device(initial, diffusivity, forcing, guessed):
    p = lax.axis_index("tm")
    y = lax.axis_index("space")
    ny = lax.axis_size("space")
    rows, columns = diffusivity.shape
    z, x, c = p // 8, (p // 2) % 4, p % 2
    h = x // 2
    odd = x % 2 == 1
    upper = odd != (h == 1)
    core0 = c == 0
    zero = jnp.float32(0)

    sources = forcing.reshape((FACTOR, FACTOR) + forcing.shape[1:])
    first = jnp.where(p == 0, initial, zero)[None]
    above = shift(diffusivity[rows - E :], "space", 1)
    below = shift(diffusivity[:E], "space", -1)

    cur = wide(jnp.concatenate([first, guessed], 0), 8)
    src = wide(sources, 8)
    above, below, cur = hold(above, below, cur)
    above = jnp.where(y == 0, zero, above)
    below = jnp.where(y == ny - 1, zero, below)
    dwide = jnp.concatenate([above, diffusivity, below], 0)

    def dext(e):
        return dwide[E - e : E + rows + e]

    for i in range(FACTOR):
        cur = step(cur, dext(8), S0)
        cur = jnp.concatenate([cur[:4] + src[:, i], cur[4:]], 0)
    relaxed, gw = cur[:4], cur[4]
    d = relaxed - wide(guessed, 8)
    dw = regrow(d, 8, 16)
    gw16 = regrow(gw, 8, 16)
    d16 = dext(16)
    xf = step(dw[0], d16, S1) + dw[1]
    xf = step(xf, d16, S1) + dw[2]
    yf = steps(step(dw[3], d16, S1) + gw16, d16, S1, 2)
    xy = steps(jnp.stack([xf, yf]), d16, S0, 4)
    xy, dheld = hold(xy, dwide)
    d24 = dext(24)
    own = steps(regrow(d[:2], 8, 24), d24, S0, 2)
    theirs, own = hold(swap(xy, 1), own)

    dpad = edged(dheld)
    dhalf = jnp.where(core0, dpad[:, :384], dpad[:, 256:])
    dquarter = jnp.where(upper, dhalf[:, 128:], dhalf[:, :256])

    def half(v):
        w = edged(v)
        return jnp.where(core0, w[..., :384], w[..., 256:])

    mine_h, theirs_h = half(xy), half(theirs)
    x0 = jnp.where(core0, mine_h[0], theirs_h[0])
    x1 = jnp.where(core0, theirs_h[0], mine_h[0])
    y0 = jnp.where(core0, mine_h[1], theirs_h[1])
    y1 = jnp.where(core0, theirs_h[1], mine_h[1])
    r = x1 + y0
    dh = dhalf[E - 16 : E + rows + 16]
    t = step(jnp.where(odd, r, x0), dh, S2) + jnp.where(odd, y1, r)
    t = step(t, dh, S2)
    f1 = jnp.where(odd, x0, t + y1)
    f2 = jnp.where(odd, step(t, dh, S2), zero)
    xy0 = jnp.where(core0, xy, theirs)
    xy1 = jnp.where(core0, theirs, xy)
    rfull = xy1[0] + xy0[1]
    rfull_y = jnp.stack([rfull, xy1[1]])
    rpart = jnp.where(core0, rfull_y[:, :48], rfull_y[:, 48:])
    ff, own, d3gw, rpart = hold(
        jnp.stack([f1, f2]), own, jnp.stack([d[3], gw])[:, 4:-4], rpart
    )
    keep = jnp.where(upper, ff[..., 128:], ff[..., :256])
    give = jnp.where(upper, ff[..., :256], ff[..., 128:])
    def r24(v):
        return regrow(v, 16, 24)

    own = steps(own, d24, S0, 2)
    other, own = hold(swap(give, 2), own)
    keep = keep + other

    def dq(e):
        return dquarter[E - e : E + rows + e]

    def to_psi(v):
        g = step(v[0], dq(16), S3) + v[1]
        return jnp.where(low, step(g, dq(16), S3), g)

    low = h == 0
    psi = to_psi(keep)
    before, after, rpart, d3gw = hold(
        shift(keep, "tm", 8),
        shift(psi, "tm", -8),
        shift(rpart, "tm", 2),
        shift(d3gw, "tm", 1),
    )
    before = jnp.where(z >= 1, before, zero)
    last = z == 7
    u = steps(regrow(to_psi(before), 16, 20), dq(20), S3, 2) + regrow(psi, 16, 20)
    u = jnp.where(last, zero, steps(u, dq(20), S3, 2)) + regrow(after, 16, 20)

    q0 = (z == 0) & (x == 0)
    d3gw = regrow(jnp.where(p == 0, zero, d3gw), 4, 16)
    rpart = jnp.where(q0, zero, rpart)
    dz = dq(32)
    bw, kw = regrow(before, 16, 32), regrow(keep, 16, 32)
    eps = jnp.where(low, bw[0], zero)
    tau = jnp.where(low, bw[1], bw[0])
    tau1 = jnp.where(low, kw[0], bw[1])
    tau2 = jnp.where(low, kw[1], kw[0])
    eps1 = step(eps, dz, S3) + tau
    eps2 = step(eps1, dz, S3) + tau1
    near = steps(jnp.stack([eps, eps1, eps2]), dz, S2, 4) + jnp.stack([tau, tau1, tau2])
    sent = steps(r24(d3gw), d24, S0, 4)
    u3raw = shift(u, "tm", 24)
    u6, ry2, near, sent = hold(shift(u, "tm", -16), swap(rpart, 1), near, sent)
    ry = jnp.where(
        core0, jnp.concatenate([rpart, ry2], 1), jnp.concatenate([ry2, rpart], 1)
    )
    rp, yp = ry[0], ry[1]
    s1 = step(rp, d16, S2) + xy0[0] + yp
    s1 = jnp.where(core0, s1[:, :256], s1[:, 256:])
    u6 = steps(jnp.where(z >= 5, regrow(u6, 20, 32), zero), dz, S3, 6)
    u3, u6 = hold(u3raw, u6)
    u3 = jnp.where(z >= 2, u3, zero)
    far = regrow(u3, 20, 32) + u6
    far = steps(far, dz, S2, 4)
    far1 = step(far, dz, S3)
    zs = near + jnp.stack([far, far1, step(far1, dz, S3)])
    zs = zs[..., EDGE:-EDGE]
    keep = jnp.where(low, zs[:2], zs[1:])
    give = jnp.where(low, zs[1:], zs[:2])

    gwp = r24(d3gw[1])
    a3p, a0, a1 = sent[0], own[0] + sent[1], own[1]
    rprev = jnp.where(core0, r24(rp), r24(xy0[0] + yp))
    rown = jnp.where(core0, r24(xy0[0] + yp), r24(rfull))
    ea = jnp.where(core0, zero, r24(rp))
    eb = step(ea, d24, S2) + rprev
    eb = jnp.where(odd & (c == 1), zero, eb)
    pair = steps(jnp.stack([ea, eb]), d24, S1, 4)
    y_1 = step(rprev + pair[0], d24, S1) + a3p
    y_2 = step(y_1, d24, S1) + a0
    y_3 = step(y_2, d24, S1) + a1
    rel = regrow(relaxed, 8, 24)
    local = jnp.stack([rel[0] + gwp + y_1, rel[1] + y_2, rel[2] + y_3, rel[3] + rown + pair[1]])

    other, s1x, local = hold(swap(give, 6), swap(s1, 2), local)
    keep = keep + other
    s1x = jnp.where(odd, s1x, zero)

    n = rows + 2 * E

    m = rows + 48

    def packed(v, w):
        return jnp.concatenate([v[0, :24], v[0, 24:], v[1, :24], v[1, 24:], w], 1)

    def unpacked(v):
        z0 = jnp.concatenate([v[:, :128], v[:, 128:256]], 0)
        z1 = jnp.concatenate([v[:, 256:384], v[:, 384:512]], 0)
        return jnp.stack([z0, z1]), v[:, 512:]

    from_above, from_below = hold(
        shift(packed(keep[:, n - 48 :], s1x[-24:]), "space", 1),
        shift(packed(keep[:, :48], s1x[:24]), "space", -1),
    )
    from_above = jnp.where(y == 0, zero, from_above)
    from_below = jnp.where(y == ny - 1, zero, from_below)
    za, sa = unpacked(from_above)
    zb, sb = unpacked(from_below)
    keep = keep[:, 16:-16] + jnp.concatenate([za, zb], 1)
    s1g = s1x + jnp.pad(sa, ((8, 64), (0, 0))) + jnp.pad(sb, ((64, 8), (0, 0)))
    other, la, lb = hold(
        swap(keep, 2), shift(local[:, m - 24 :], "space", 1), shift(local[:, :24], "space", -1)
    )
    la = jnp.where(y == 0, zero, la)
    lb = jnp.where(y == ny - 1, zero, lb)
    keep = jnp.where(upper, jnp.concatenate([other, keep], 2), jnp.concatenate([keep, other], 2))
    keep = jnp.concatenate([keep, s1g[None]], 0)
    other = swap(keep, 1)
    both = jnp.where(
        core0, jnp.concatenate([keep, other], 2), jnp.concatenate([other, keep], 2)
    )
    d8 = dext(8)
    q = jnp.where(odd, steps(both[0], d16, S2, 2) + both[2], both[0])[8:-8]
    both = steps(jnp.stack([q, both[1, 8:-8]]), d8, S1, 4)
    q, zn = both[0], both[1]
    q = jnp.where(core0, q, step(q, d8, S2))
    e2b = jnp.where(odd & (c == 1), zn, step(q, d8, S2))
    t1 = step(q, d8, S1)
    t2 = step(t1, d8, S1)
    t3 = step(t2, d8, S1)
    correction = jnp.stack([t1, t2, t3, e2b])[:, 8:-8]

    inner = local[:, 24:-24]
    inner = (
        inner
        + jnp.pad(la, ((0, 0), (0, rows - 24), (0, 0)))
        + jnp.pad(lb, ((0, 0), (rows - 24, 0), (0, 0)))
    )
    return inner + correction


def solution(mesh):
    return jax.shard_map(
        per_device,
        mesh=mesh,
        in_specs=(
            P("space", None),
            P("space", None),
            P("tm", "space", None),
            P("tm", "space", None),
        ),
        out_specs=P("tm", "space", None),
        check_vma=False,
    )
```

```python
import jax
import jax.numpy as jnp
from jax import lax
from jax.sharding import PartitionSpec as P

FACTOR = 4
E = 32
EDGE = 32
S0, S1, S2, S3 = 1.0, 4.0, 16.0, 64.0


def wide(v, e):
    return jnp.pad(v, [(0, 0)] * (v.ndim - 2) + [(e, e), (0, 0)])


def regrow(v, before, after):
    return wide(v, after - before)


def edged(v):
    return jnp.pad(v, [(0, 0)] * (v.ndim - 1) + [(EDGE, EDGE)])


def shift(v, axis, by):
    n = lax.axis_size(axis)
    return lax.ppermute(v, axis, [(i, (i + by) % n) for i in range(n)])


def swap(v, bit):
    n = lax.axis_size("tm")
    return lax.ppermute(v, "tm", [(i, i ^ bit) for i in range(n)])


def hold(*values):
    return lax.optimization_barrier(values)


def thin(v):
    r = v.shape[-2]
    k = -(-r // 16) * 8
    tail = jnp.concatenate([v[..., :k, 128:], v[..., r - k :, 128:]], -1)
    return jnp.concatenate([v[..., :128], tail], -2)


def thick(m, r):
    k = -(-r // 16) * 8
    low, high = m[..., r:, :64], m[..., r + 2 * k - r :, 64:]
    return jnp.concatenate([m[..., :r, :], jnp.concatenate([low, high], -2)], -1)


def step(v, d, s):
    q = jnp.pad(v, [(0, 0)] * (v.ndim - 2) + [(1, 1), (1, 1)])
    lap = q[..., 2:, 1:-1] + q[..., :-2, 1:-1] + q[..., 1:-1, 2:] + q[..., 1:-1, :-2] - 4.0 * v
    return v + (s * d) * lap


def steps(v, d, s, k):
    for _ in range(k):
        v = step(v, d, s)
    return v


def per_device(initial, diffusivity, forcing, guessed):
    p = lax.axis_index("tm")
    y = lax.axis_index("space")
    ny = lax.axis_size("space")
    rows, columns = diffusivity.shape
    z, x, c = p // 8, (p // 2) % 4, p % 2
    h = x // 2
    odd = x % 2 == 1
    upper = odd != (h == 1)
    core0 = c == 0
    zero = jnp.float32(0)

    sources = forcing.reshape((FACTOR, FACTOR) + forcing.shape[1:])
    first = jnp.where(p == 0, initial, zero)[None]
    above = shift(diffusivity[rows - E :], "space", 1)
    below = shift(diffusivity[:E], "space", -1)

    cur = wide(jnp.concatenate([first, guessed], 0), 8)
    src = wide(sources, 8)
    above, below, cur = hold(above, below, cur)
    above = jnp.where(y == 0, zero, above)
    below = jnp.where(y == ny - 1, zero, below)
    dwide = jnp.concatenate([above, diffusivity, below], 0)

    def dext(e):
        return dwide[E - e : E + rows + e]

    for i in range(FACTOR):
        cur = step(cur, dext(8), S0)
        cur = jnp.concatenate([cur[:4] + src[:, i], cur[4:]], 0)
    relaxed, gw = cur[:4], cur[4]
    d = relaxed - wide(guessed, 8)
    dw = regrow(d, 8, 16)
    gw16 = regrow(gw, 8, 16)
    d16 = dext(16)
    xf = step(dw[0], d16, S1) + dw[1]
    xf = step(xf, d16, S1) + dw[2]
    yf = steps(step(dw[3], d16, S1) + gw16, d16, S1, 2)
    xy = steps(jnp.stack([xf, yf]), d16, S0, 4)
    xy, dheld = hold(xy, dwide)
    d24 = dext(24)
    own = steps(regrow(d[:2], 8, 24), d24, S0, 2)
    theirs, own = hold(swap(xy, 1), own)

    dpad = edged(dheld)
    dhalf = jnp.where(core0, dpad[:, :320], dpad[:, 256:])
    dquarter = jnp.where(upper, dhalf[:, 128:], dhalf[:, :192])

    def half(v):
        w = edged(v)
        return jnp.where(core0, w[..., :320], w[..., 256:])

    mine_h, theirs_h = half(xy), half(theirs)
    x0 = jnp.where(core0, mine_h[0], theirs_h[0])
    x1 = jnp.where(core0, theirs_h[0], mine_h[0])
    y0 = jnp.where(core0, mine_h[1], theirs_h[1])
    y1 = jnp.where(core0, theirs_h[1], mine_h[1])
    r = x1 + y0
    dh = dhalf[E - 16 : E + rows + 16]
    t = step(jnp.where(odd, r, x0), dh, S2) + jnp.where(odd, y1, r)
    t = step(t, dh, S2)
    f1 = jnp.where(odd, x0, t + y1)
    f2 = jnp.where(odd, step(t, dh, S2), zero)
    xy0 = jnp.where(core0, xy, theirs)
    xy1 = jnp.where(core0, theirs, xy)
    rfull = xy1[0] + xy0[1]
    rfull_y = jnp.stack([rfull, xy1[1]])
    rpart = jnp.where(core0, rfull_y[:, :48], rfull_y[:, 48:])
    ff, own, d3gw, rpart = hold(
        jnp.stack([f1, f2]), own, jnp.stack([d[3], gw])[:, 4:-4], rpart
    )
    keep = jnp.where(upper, ff[..., 128:], ff[..., :192])
    give = jnp.where(upper, ff[..., :192], ff[..., 128:])
    def r24(v):
        return regrow(v, 16, 24)

    own = steps(own, d24, S0, 2)
    other, own, packed_keep = hold(swap(thin(give), 2), own, thin(keep))
    packed_keep = packed_keep + other
    keep = thick(packed_keep, 96)

    def dq(e):
        return dquarter[E - e : E + rows + e]

    def to_psi(v):
        g = step(v[0], dq(16), S3) + v[1]
        return jnp.where(low, step(g, dq(16), S3), g)

    low = h == 0
    psi = to_psi(keep)
    before, after, rpart, d3gw = hold(
        shift(packed_keep, "tm", 8),
        shift(thin(psi), "tm", -8),
        shift(rpart, "tm", 2),
        shift(d3gw, "tm", 1),
    )
    before = jnp.where(z >= 1, thick(before, 96), zero)
    after = thick(after, 96)
    last = z == 7
    u = steps(regrow(to_psi(before), 16, 20), dq(20), S3, 2) + regrow(psi, 16, 20)
    u = jnp.where(last, zero, steps(u, dq(20), S3, 2)) + regrow(after, 16, 20)

    q0 = (z == 0) & (x == 0)
    d3gw = regrow(jnp.where(p == 0, zero, d3gw), 4, 16)
    rpart = jnp.where(q0, zero, rpart)
    dz = dq(32)
    bw, kw = regrow(before, 16, 32), regrow(keep, 16, 32)
    eps = jnp.where(low, bw[0], zero)
    tau = jnp.where(low, bw[1], bw[0])
    tau1 = jnp.where(low, kw[0], bw[1])
    tau2 = jnp.where(low, kw[1], kw[0])
    eps1 = step(eps, dz, S3) + tau
    eps2 = step(eps1, dz, S3) + tau1
    near = steps(jnp.stack([eps, eps1, eps2]), dz, S2, 4) + jnp.stack([tau, tau1, tau2])
    sent = steps(r24(d3gw), d24, S0, 4)
    u3raw = shift(thin(u), "tm", 24)
    u6, ry2, near, sent = hold(shift(thin(u), "tm", -16), swap(rpart, 1), near, sent)
    ry = jnp.where(
        core0, jnp.concatenate([rpart, ry2], 1), jnp.concatenate([ry2, rpart], 1)
    )
    rp, yp = ry[0], ry[1]
    s1 = step(rp, d16, S2) + xy0[0] + yp
    s1 = jnp.where(core0, s1[:, :256], s1[:, 256:])
    u6 = steps(jnp.where(z >= 5, regrow(thick(u6, 104), 20, 32), zero), dz, S3, 6)
    u3, u6 = hold(u3raw, u6)
    u3 = jnp.where(z >= 2, thick(u3, 104), zero)
    far = regrow(u3, 20, 32) + u6
    far = steps(far, dz, S2, 4)
    far1 = step(far, dz, S3)
    zs = near + jnp.stack([far, far1, step(far1, dz, S3)])
    zs = zs[..., EDGE:-EDGE]
    keep = jnp.where(low, zs[:2], zs[1:])
    give = jnp.where(low, zs[1:], zs[:2])

    gwp = r24(d3gw[1])
    a3p, a0, a1 = sent[0], own[0] + sent[1], own[1]
    rprev = jnp.where(core0, r24(rp), r24(xy0[0] + yp))
    rown = jnp.where(core0, r24(xy0[0] + yp), r24(rfull))
    ea = jnp.where(core0, zero, r24(rp))
    eb = step(ea, d24, S2) + rprev
    eb = jnp.where(odd & (c == 1), zero, eb)
    pair = steps(jnp.stack([ea, eb]), d24, S1, 4)
    y_1 = step(rprev + pair[0], d24, S1) + a3p
    y_2 = step(y_1, d24, S1) + a0
    y_3 = step(y_2, d24, S1) + a1
    rel = regrow(relaxed, 8, 24)
    local = jnp.stack([rel[0] + gwp + y_1, rel[1] + y_2, rel[2] + y_3, rel[3] + rown + pair[1]])

    other, s1x, local = hold(swap(give, 6), swap(s1, 2), local)
    keep = keep + other
    s1x = jnp.where(odd, s1x, zero)

    n = rows + 2 * E

    m = rows + 48

    def packed(v, w):
        return jnp.concatenate([v[0, :24], v[0, 24:], v[1, :24], v[1, 24:], w], 1)

    def unpacked(v):
        z0 = jnp.concatenate([v[:, :128], v[:, 128:256]], 0)
        z1 = jnp.concatenate([v[:, 256:384], v[:, 384:512]], 0)
        return jnp.stack([z0, z1]), v[:, 512:]

    from_above, from_below = hold(
        shift(packed(keep[:, n - 48 :], s1x[-24:]), "space", 1),
        shift(packed(keep[:, :48], s1x[:24]), "space", -1),
    )
    from_above = jnp.where(y == 0, zero, from_above)
    from_below = jnp.where(y == ny - 1, zero, from_below)
    za, sa = unpacked(from_above)
    zb, sb = unpacked(from_below)
    keep = keep[:, 16:-16] + jnp.concatenate([za, zb], 1)
    s1g = s1x + jnp.pad(sa, ((8, 64), (0, 0))) + jnp.pad(sb, ((64, 8), (0, 0)))
    other, la, lb = hold(
        swap(keep, 2), shift(local[:, m - 24 :], "space", 1), shift(local[:, :24], "space", -1)
    )
    la = jnp.where(y == 0, zero, la)
    lb = jnp.where(y == ny - 1, zero, lb)
    keep = jnp.where(upper, jnp.concatenate([other, keep], 2), jnp.concatenate([keep, other], 2))
    keep = jnp.concatenate([keep, s1g[None]], 0)
    other = swap(keep, 1)
    both = jnp.where(
        core0, jnp.concatenate([keep, other], 2), jnp.concatenate([other, keep], 2)
    )
    d8 = dext(8)
    q = jnp.where(odd, steps(both[0], d16, S2, 2) + both[2], both[0])[8:-8]
    both = steps(jnp.stack([q, both[1, 8:-8]]), d8, S1, 4)
    q, zn = both[0], both[1]
    q = jnp.where(core0, q, step(q, d8, S2))
    e2b = jnp.where(odd & (c == 1), zn, step(q, d8, S2))
    t1 = step(q, d8, S1)
    t2 = step(t1, d8, S1)
    t3 = step(t2, d8, S1)
    correction = jnp.stack([t1, t2, t3, e2b])[:, 8:-8]

    inner = local[:, 24:-24]
    inner = (
        inner
        + jnp.pad(la, ((0, 0), (0, rows - 24), (0, 0)))
        + jnp.pad(lb, ((0, 0), (rows - 24, 0), (0, 0)))
    )
    return inner + correction


def solution(mesh):
    return jax.shard_map(
        per_device,
        mesh=mesh,
        in_specs=(
            P("space", None),
            P("space", None),
            P("tm", "space", None),
            P("tm", "space", None),
        ),
        out_specs=P("tm", "space", None),
        check_vma=False,
    )
```

```python
import jax
import jax.numpy as jnp
from jax import lax
from jax.sharding import PartitionSpec as P

FACTOR = 4
E = 32
EDGE = 32
S0, S1, S2, S3 = 1.0, 4.0, 16.0, 64.0


def wide(v, e):
    return jnp.pad(v, [(0, 0)] * (v.ndim - 2) + [(e, e), (0, 0)])


def regrow(v, before, after):
    return wide(v, after - before)


def edged(v):
    return jnp.pad(v, [(0, 0)] * (v.ndim - 1) + [(EDGE, EDGE)])


def shift(v, axis, by):
    n = lax.axis_size(axis)
    return lax.ppermute(v, axis, [(i, (i + by) % n) for i in range(n)])


def swap(v, bit):
    n = lax.axis_size("tm")
    return lax.ppermute(v, "tm", [(i, i ^ bit) for i in range(n)])


def hold(*values):
    return lax.optimization_barrier(values)


def thin(v):
    r = v.shape[-2]
    k = -(-r // 16) * 8
    tail = jnp.concatenate([v[..., :k, 128:], v[..., r - k :, 128:]], -1)
    return jnp.concatenate([v[..., :128], tail], -2)


def thick(m, r):
    k = -(-r // 16) * 8
    low, high = m[..., r:, :64], m[..., r + 2 * k - r :, 64:]
    return jnp.concatenate([m[..., :r, :], jnp.concatenate([low, high], -2)], -1)


def step(v, d, s):
    q = jnp.pad(v, [(0, 0)] * (v.ndim - 2) + [(1, 1), (1, 1)])
    lap = q[..., 2:, 1:-1] + q[..., :-2, 1:-1] + q[..., 1:-1, 2:] + q[..., 1:-1, :-2] - 4.0 * v
    return v + (s * d) * lap


def steps(v, d, s, k):
    for _ in range(k):
        v = step(v, d, s)
    return v


def per_device(initial, diffusivity, forcing, guessed):
    p = lax.axis_index("tm")
    y = lax.axis_index("space")
    ny = lax.axis_size("space")
    rows, columns = diffusivity.shape
    z, x, c = p // 8, (p // 2) % 4, p % 2
    h = x // 2
    odd = x % 2 == 1
    upper = odd != (h == 1)
    core0 = c == 0
    zero = jnp.float32(0)

    sources = forcing.reshape((FACTOR, FACTOR) + forcing.shape[1:])
    first = jnp.where(p == 0, initial, zero)[None]
    above = shift(diffusivity[rows - E :], "space", 1)
    below = shift(diffusivity[:E], "space", -1)

    cur = wide(jnp.concatenate([first, guessed], 0), 8)
    src = wide(sources, 8)
    above, below, cur = hold(above, below, cur)
    above = jnp.where(y == 0, zero, above)
    below = jnp.where(y == ny - 1, zero, below)
    dwide = jnp.concatenate([above, diffusivity, below], 0)

    def dext(e):
        return dwide[E - e : E + rows + e]

    for i in range(FACTOR):
        cur = step(cur, dext(8), S0)
        cur = jnp.concatenate([cur[:4] + src[:, i], cur[4:]], 0)
    relaxed, gw = cur[:4], cur[4]
    d = relaxed - wide(guessed, 8)
    dw = regrow(d, 8, 16)
    gw16 = regrow(gw, 8, 16)
    d16 = dext(16)
    xf = step(dw[0], d16, S1) + dw[1]
    xf = step(xf, d16, S1) + dw[2]
    yf = steps(step(dw[3], d16, S1) + gw16, d16, S1, 2)
    xy = steps(jnp.stack([xf, yf]), d16, S0, 4)
    xy, dheld = hold(xy, dwide)
    d24 = dext(24)
    own = steps(regrow(d[:2], 8, 24), d24, S0, 3)
    theirs, own = hold(swap(xy, 1), own)

    dpad = edged(dheld)
    dhalf = jnp.where(core0, dpad[:, :320], dpad[:, 256:])
    dquarter = jnp.where(upper, dhalf[:, 128:], dhalf[:, :192])

    def half(v):
        w = edged(v)
        return jnp.where(core0, w[..., :320], w[..., 256:])

    mine_h, theirs_h = half(xy), half(theirs)
    x0 = jnp.where(core0, mine_h[0], theirs_h[0])
    x1 = jnp.where(core0, theirs_h[0], mine_h[0])
    y0 = jnp.where(core0, mine_h[1], theirs_h[1])
    y1 = jnp.where(core0, theirs_h[1], mine_h[1])
    r = x1 + y0
    dh = dhalf[E - 16 : E + rows + 16]
    t = step(jnp.where(odd, r, x0), dh, S2) + jnp.where(odd, y1, r)
    t = step(t, dh, S2)
    f1 = jnp.where(odd, x0, t + y1)
    f2 = jnp.where(odd, step(t, dh, S2), zero)
    xy0 = jnp.where(core0, xy, theirs)
    xy1 = jnp.where(core0, theirs, xy)
    rfull = xy1[0] + xy0[1]
    rfull_y = jnp.stack([rfull, xy1[1]])
    rpart = jnp.where(core0, rfull_y[:, :48], rfull_y[:, 48:])
    ff, own, d3gw, rpart = hold(
        jnp.stack([f1, f2]), own, jnp.stack([d[3], gw])[:, 4:-4], rpart
    )
    keep = jnp.where(upper, ff[..., 128:], ff[..., :192])
    give = jnp.where(upper, ff[..., :192], ff[..., 128:])
    def r24(v):
        return regrow(v, 16, 24)

    own = step(own, d24, S0)
    other, own, packed_keep = hold(swap(thin(give), 2), own, thin(keep))
    packed_keep = packed_keep + other
    keep = thick(packed_keep, 96)

    def dq(e):
        return dquarter[E - e : E + rows + e]

    def to_psi(v):
        g = step(v[0], dq(16), S3) + v[1]
        return jnp.where(low, step(g, dq(16), S3), g)

    low = h == 0
    psi = to_psi(keep)
    before, after, rpart, d3gw = hold(
        shift(packed_keep, "tm", 8),
        shift(thin(psi), "tm", -8),
        shift(rpart, "tm", 2),
        shift(d3gw, "tm", 1),
    )
    before = jnp.where(z >= 1, thick(before, 96), zero)
    after = thick(after, 96)
    last = z == 7
    u = steps(regrow(to_psi(before), 16, 20), dq(20), S3, 2) + regrow(psi, 16, 20)
    u = jnp.where(last, zero, steps(u, dq(20), S3, 2)) + regrow(after, 16, 20)

    q0 = (z == 0) & (x == 0)
    d3gw = regrow(jnp.where(p == 0, zero, d3gw), 4, 16)
    rpart = jnp.where(q0, zero, rpart)
    dz = dq(32)
    bw, kw = regrow(before, 16, 32), regrow(keep, 16, 32)
    eps = jnp.where(low, bw[0], zero)
    tau = jnp.where(low, bw[1], bw[0])
    tau1 = jnp.where(low, kw[0], bw[1])
    tau2 = jnp.where(low, kw[1], kw[0])
    eps1 = step(eps, dz, S3) + tau
    eps2 = step(eps1, dz, S3) + tau1
    near = steps(jnp.stack([eps, eps1, eps2]), dz, S2, 4) + jnp.stack([tau, tau1, tau2])
    sent = steps(r24(d3gw), d24, S0, 4)
    u3raw = shift(thin(u), "tm", 24)
    u6, ry2, near, sent = hold(shift(thin(u), "tm", -16), swap(rpart, 1), near, sent)
    ry = jnp.where(
        core0, jnp.concatenate([rpart, ry2], 1), jnp.concatenate([ry2, rpart], 1)
    )
    rp, yp = ry[0], ry[1]
    s1 = step(rp, d16, S2) + xy0[0] + yp
    s1 = jnp.where(core0, s1[:, :256], s1[:, 256:])
    u6 = steps(jnp.where(z >= 5, regrow(thick(u6, 104), 20, 32), zero), dz, S3, 6)
    u3, u6 = hold(u3raw, u6)
    u3 = jnp.where(z >= 2, thick(u3, 104), zero)
    far = regrow(u3, 20, 32) + u6
    far = steps(far, dz, S2, 4)
    far1 = step(far, dz, S3)
    zs = near + jnp.stack([far, far1, step(far1, dz, S3)])
    zs = zs[..., EDGE:-EDGE]
    keep = jnp.where(low, zs[:2], zs[1:])
    give = jnp.where(low, zs[1:], zs[:2])

    gwp = r24(d3gw[1])
    a3p, a0, a1 = sent[0], own[0] + sent[1], own[1]
    rprev = jnp.where(core0, r24(rp), r24(xy0[0] + yp))
    rown = jnp.where(core0, r24(xy0[0] + yp), r24(rfull))
    ea = jnp.where(core0, zero, r24(rp))
    eb = step(ea, d24, S2) + rprev
    eb = jnp.where(odd & (c == 1), zero, eb)
    pair = steps(jnp.stack([ea, eb]), d24, S1, 4)
    y_1 = step(rprev + pair[0], d24, S1) + a3p
    y_2 = step(y_1, d24, S1) + a0
    y_3 = step(y_2, d24, S1) + a1
    rel = regrow(relaxed, 8, 24)
    local = jnp.stack([rel[0] + gwp + y_1, rel[1] + y_2, rel[2] + y_3, rel[3] + rown + pair[1]])

    other, s1x, local = hold(swap(give, 6), swap(s1, 2), local)
    keep = keep + other
    s1x = jnp.where(odd, s1x, zero)

    n = rows + 2 * E

    m = rows + 48

    def packed(v, w):
        return jnp.concatenate([v[0, :24], v[0, 24:], v[1, :24], v[1, 24:], w], 1)

    def unpacked(v):
        z0 = jnp.concatenate([v[:, :128], v[:, 128:256]], 0)
        z1 = jnp.concatenate([v[:, 256:384], v[:, 384:512]], 0)
        return jnp.stack([z0, z1]), v[:, 512:]

    from_above, from_below = hold(
        shift(packed(keep[:, n - 48 :], s1x[-24:]), "space", 1),
        shift(packed(keep[:, :48], s1x[:24]), "space", -1),
    )
    from_above = jnp.where(y == 0, zero, from_above)
    from_below = jnp.where(y == ny - 1, zero, from_below)
    za, sa = unpacked(from_above)
    zb, sb = unpacked(from_below)
    keep = keep[:, 16:-16] + jnp.concatenate([za, zb], 1)
    s1g = s1x + jnp.pad(sa, ((8, 64), (0, 0))) + jnp.pad(sb, ((64, 8), (0, 0)))
    other, la, lb = hold(
        swap(keep, 2), shift(local[:, m - 24 :], "space", 1), shift(local[:, :24], "space", -1)
    )
    la = jnp.where(y == 0, zero, la)
    lb = jnp.where(y == ny - 1, zero, lb)
    keep = jnp.where(upper, jnp.concatenate([other, keep], 2), jnp.concatenate([keep, other], 2))
    keep = jnp.concatenate([keep, s1g[None]], 0)
    other = swap(keep, 1)
    both = jnp.where(
        core0, jnp.concatenate([keep, other], 2), jnp.concatenate([other, keep], 2)
    )
    d8 = dext(8)
    q = jnp.where(odd, steps(both[0], d16, S2, 2) + both[2], both[0])[8:-8]
    both = steps(jnp.stack([q, both[1, 8:-8]]), d8, S1, 4)
    q, zn = both[0], both[1]
    q = jnp.where(core0, q, step(q, d8, S2))
    e2b = jnp.where(odd & (c == 1), zn, step(q, d8, S2))
    t1 = step(q, d8, S1)
    t2 = step(t1, d8, S1)
    t3 = step(t2, d8, S1)
    correction = jnp.stack([t1, t2, t3, e2b])[:, 8:-8]

    inner = local[:, 24:-24]
    inner = (
        inner
        + jnp.pad(la, ((0, 0), (0, rows - 24), (0, 0)))
        + jnp.pad(lb, ((0, 0), (rows - 24, 0), (0, 0)))
    )
    return inner + correction


def solution(mesh):
    return jax.shard_map(
        per_device,
        mesh=mesh,
        in_specs=(
            P("space", None),
            P("space", None),
            P("tm", "space", None),
            P("tm", "space", None),
        ),
        out_specs=P("tm", "space", None),
        check_vma=False,
    )
```
